32 devices in a mesh: date: 4 (over y, x), az: 8 (over z, core).
Axes of the slice: x: 2, y: 2, z: 4, core: 2. Of those that a mesh axis runs over, the one named last changes fastest.
Arguments:
- epoch_image_tensor: bfloat16 [16, 2, 2560, 1280], P('date', None, 'az'), may hold values from -5 to 5
- along_track_shifts: int32 [16, 40, 20], P('date', 'az'), may hold values from -32 to 32, as said below
- cross_track_shifts: int32 [16, 40, 20], P('date', 'az'), may hold values from -32 to 32, as said below
- epoch_present_table: int32 [16, 40], P('date', 'az'), may hold values 0 or 1
Outputs:
- tile_similarity: float32 [16, 40, 20], P('date', 'az')
- smoothed_ifgs: float32 [16, 2, 512, 64], P('date', None, 'az')
The draws below stay inside these ranges and needn't reach their ends.
Inputs may be any that keep to these rules, and one draw needn't show every extreme that they name: `along_track_shifts`: date 0 has all offsets zero. `cross_track_shifts`: date 0 has all offsets zero.
All inputs are finite; a program needn't handle non-finite values. Where the reference program divides by a largest or mean magnitude, that divisor is 1e-20 or more. No bound on the sum of `epoch_present_table` on one device may be relied on, other than what follows from the above.
Results may differ from the reference program's by a relative error of at most 0.0003.
Values may be sent and summed in bfloat16 or wider, within the bound.
A program may use at most 192 MiB of HBM per device.

```python
import jax
import jax.numpy as jnp
from jax import lax

RG = 1280
WIN = 64
MARGIN_LINES = 32
RHALO = 32
LOOK_AZ = 5
LOOK_RG = 20
PATCH = 32
EPOCH_COUNT = 16
AZ = 2560
TILES_ALONG = 40
MA = 512
MR = 64


def shift_fields(key):
    tensor_extent = (EPOCH_COUNT, AZ // WIN, RG // WIN)
    shift_rows = jax.random.randint(jax.random.fold_in(key, 11), tensor_extent, -MARGIN_LINES, MARGIN_LINES + 1)
    shift_cols = jax.random.randint(jax.random.fold_in(key, 12), tensor_extent, -RHALO, RHALO + 1)
    later = (jnp.arange(EPOCH_COUNT) > 0).astype(jnp.int32)[:, None, None]
    return ((shift_rows * later).astype(jnp.int32), (shift_cols * later).astype(jnp.int32))


def draw_along_track_shifts(key, part):
    return shift_fields(key)[0]


def draw_cross_track_shifts(key, part):
    return shift_fields(key)[1]


def draw_epoch_image_tensor(key, part):
    shift_rows, shift_cols = shift_fields(key)
    common = jax.random.normal(jax.random.fold_in(key, 21), (2, AZ, RG), jnp.float32)
    line_index = jnp.arange(AZ)[:, None]
    sample_index = jnp.arange(RG)[None, :]

    def lone_epoch(date_index):
        along_rows = shift_rows[date_index][line_index // WIN, sample_index // WIN]
        along_cols = shift_cols[date_index][line_index // WIN, sample_index // WIN]
        source_rows = jnp.clip(line_index - along_rows, 0, AZ - 1)
        source_cols = jnp.clip(sample_index - along_cols, 0, RG - 1)
        moved = common[:, source_rows, source_cols]
        noise = jax.random.normal(jax.random.fold_in(jax.random.fold_in(key, 23), date_index), (2, AZ, RG), jnp.float32)
        return jnp.clip(0.8 * moved + 0.6 * noise, -5.0, 5.0).astype(jnp.bfloat16)
    return lax.map(lone_epoch, jnp.arange(EPOCH_COUNT))


def with_ends(values, rng, smallest, high):
    longest = values.shape.index(max(values.shape))
    spots = []
    for shift in (0, 1):
        where = [jax.random.randint(jax.random.fold_in(rng, axis), (), 0, length) for axis, length in enumerate(values.shape)]
        where[longest] = (where[longest] + shift) % values.shape[longest]
        spots.append(tuple(where))
    return values.at[spots[0]].set(smallest).at[spots[1]].set(high)


def setup_inputs(seed: int = 0) -> dict:
    key_list = jax.random.split(jax.random.key(seed), 5)
    epoch_image_tensor = draw_epoch_image_tensor(jax.random.fold_in(key_list[4], 71), 0)
    along_track_shifts = draw_along_track_shifts(jax.random.fold_in(key_list[4], 71), 0)
    cross_track_shifts = draw_cross_track_shifts(jax.random.fold_in(key_list[4], 71), 0)
    epoch_present_table = with_ends((jax.random.randint(key_list[3], (EPOCH_COUNT, TILES_ALONG), 0, 8) < 7).astype(jnp.int32), jax.random.fold_in(key_list[3], 1), 0, 1)
    return {"epoch_image_tensor": epoch_image_tensor, "along_track_shifts": along_track_shifts, "cross_track_shifts": cross_track_shifts, "epoch_present_table": epoch_present_table}


VAR_EPS = 1e-05
RMS_EPS = 1e-06

def goldstein(looks):
    complex_looks = looks[0] + 1j * looks[1]
    patches = complex_looks.reshape(MA // PATCH, PATCH, MR // PATCH, PATCH).transpose(0, 2, 1, 3)
    spectrum = jnp.fft.fft2(patches, axes=(2, 3))
    magnitude = jnp.abs(spectrum)
    smooth = jnp.zeros_like(magnitude)
    for shift_a in (-1, 0, 1):
        for shift_b in (-1, 0, 1):
            smooth = smooth + jnp.roll(magnitude, (shift_a, shift_b), axis=(2, 3))
    weight = jnp.sqrt(smooth / 9.0)
    unscaled = jnp.fft.ifft2(spectrum * weight, axes=(2, 3)) * (PATCH * PATCH)
    power = lax.optimization_barrier(jnp.mean(jnp.abs(unscaled) ** 2, axis=(2, 3), keepdims=True))
    result = unscaled / jnp.sqrt(power + RMS_EPS)
    result = result.transpose(0, 2, 1, 3).reshape(MA, MR)
    return jnp.stack([jnp.real(result), jnp.imag(result)], axis=0)

def reference(epoch_image_tensor, along_track_shifts, cross_track_shifts, epoch_present_table):
    nwa = AZ // WIN
    nwr = RG // WIN
    primary_epoch = epoch_image_tensor[0].astype(jnp.float32)
    ref_amp = jnp.sqrt(primary_epoch[0] ** 2 + primary_epoch[1] ** 2)
    ref_win = ref_amp.reshape(nwa, WIN, nwr, WIN)
    ref_dev = ref_win - lax.optimization_barrier(jnp.mean(ref_win, axis=(1, 3), keepdims=True))
    ref_var = lax.optimization_barrier(jnp.mean(ref_dev ** 2, axis=(1, 3)))

    def lone_epoch(inputs):
        secondary, shift_rows, shift_cols, keep_flag = inputs
        padded = jnp.pad(secondary, ((0, 0), (MARGIN_LINES, MARGIN_LINES), (RHALO, RHALO)))
        row_start = (jnp.arange(nwa, dtype=jnp.int32) * WIN)[:, None] + MARGIN_LINES + shift_rows
        col_start = (jnp.arange(nwr, dtype=jnp.int32) * WIN)[None, :] + RHALO + shift_cols
        row_start = jnp.broadcast_to(row_start, (nwa, nwr)).astype(jnp.int32)
        col_start = jnp.broadcast_to(col_start, (nwa, nwr)).astype(jnp.int32)

        def cutout(start_a, start_r):
            return lax.dynamic_slice(padded, (jnp.int32(0), start_a, start_r), (2, WIN, WIN))
        tiles = jax.vmap(jax.vmap(cutout))(row_start, col_start)
        tiles = tiles * keep_flag.astype(tiles.dtype)[:, None, None, None, None]
        moved = tiles.astype(jnp.float32).transpose(2, 0, 3, 1, 4)
        sec_amp = jnp.sqrt(moved[0] ** 2 + moved[1] ** 2)
        sec_dev = sec_amp - lax.optimization_barrier(jnp.mean(sec_amp, axis=(1, 3), keepdims=True))
        sec_var = lax.optimization_barrier(jnp.mean(sec_dev ** 2, axis=(1, 3)))
        covariance = lax.optimization_barrier(jnp.mean(ref_dev * sec_dev, axis=(1, 3)))
        corr = covariance / jnp.sqrt((ref_var + VAR_EPS) * (sec_var + VAR_EPS))
        moved = moved.reshape(2, AZ, RG)
        ifg_real = primary_epoch[0] * moved[0] + primary_epoch[1] * moved[1]
        ifg_imag = primary_epoch[1] * moved[0] - primary_epoch[0] * moved[1]
        ifg = jnp.stack([ifg_real, ifg_imag], axis=0)
        looks = ifg.reshape(2, AZ // LOOK_AZ, LOOK_AZ, RG // LOOK_RG, LOOK_RG).sum(axis=(2, 4))
        return (corr, goldstein(looks))
    tile_similarity, smoothed_ifgs = lax.map(lone_epoch, (epoch_image_tensor, along_track_shifts, cross_track_shifts, epoch_present_table))
    return (tile_similarity, smoothed_ifgs)
```

```python
import functools

import jax
import jax.numpy as jnp
import numpy as np
from jax import lax
from jax.experimental import pallas as pl
from jax.experimental.pallas import tpu as pltpu
from jax.sharding import PartitionSpec as P

WIN = 64
MARGIN = 32
LOOK_AZ = 5
LOOK_RG = 20
PATCH = 32
LANES = 128

VAR_EPS = 1e-05
RMS_EPS = 1e-06
TINY = 1e-37

F32 = jnp.float32
BF16 = jnp.bfloat16


def tables(lines, samples):
    turns = np.outer(np.arange(PATCH), np.arange(PATCH)) % PATCH
    angles = turns * (2.0 * np.pi / PATCH)
    two = np.eye(2)
    cosine = np.kron(two, np.cos(angles))
    sine = np.kron(two, np.sin(angles))
    rows_fwd = np.block([[cosine, sine], [-sine, cosine]])
    cols_fwd = np.block([[cosine, -sine], [sine, cosine]])
    dft = np.stack([rows_fwd, cols_fwd]).astype(np.float32)
    near = np.abs(np.arange(PATCH)[:, None] - np.arange(PATCH)[None, :])
    circular = np.minimum(near, PATCH - near) <= 1
    four = np.eye(LANES // PATCH)
    half = np.kron(np.eye(2), np.ones((WIN, WIN)))
    blocks = np.stack(
        [half, np.kron(four, circular), np.kron(four, np.ones((PATCH, PATCH)))]
    ).astype(np.float32)
    az_pool = (
        np.arange(lines // LOOK_AZ)[:, None] == np.arange(lines)[None, :] // LOOK_AZ
    ).astype(np.float32)
    rg_pool = (
        np.arange(samples)[:, None] // LOOK_RG == np.arange(samples // LOOK_RG)[None, :]
    ).astype(np.float32)
    rg_pool = np.concatenate([rg_pool, rg_pool], axis=0)
    return (
        jnp.asarray(dft),
        jnp.asarray(blocks, BF16),
        jnp.asarray(az_pool, BF16),
        jnp.asarray(rg_pool, BF16),
    )


def dot(a, b):
    return jnp.dot(a, b, preferred_element_type=F32)


def dot_high(a, b):
    return jnp.dot(a, b, preferred_element_type=F32, precision=lax.Precision.HIGHEST)


def split(x):
    high = x.astype(BF16)
    return high, (x - high.astype(F32)).astype(BF16)


def dot_right(x, ones):
    high, low = split(x)
    return dot(high, ones) + dot(low, ones)


def dot_left(ones, x):
    high, low = split(x)
    return dot(ones, high) + dot(ones, low)


def root(x):
    return x * lax.rsqrt(jnp.maximum(x, TINY))


def window_row(p, sizes, at_ref, ct_ref, pr_ref, ref_chunk, blk_ref, rgp_ref, wide, band, prod, pooled, stats, sims):
    dates, lines, strips = sizes
    for m in range(strips):
        cols = slice(m * LANES, (m + 1) * LANES)
        real = ref_chunk(0, cols)
        imag = ref_chunk(1, cols)
        band[0, m] = real
        band[1, m] = imag
        amp = root(real * real + imag * imag).reshape(WIN // 8, 8, LANES)
        mean = jnp.sum(amp, axis=0) * (8.0 / WIN)
        dev = amp - mean[None]
        band[2, m] = dev.reshape(WIN, LANES)
        stats[0, m, dates] = mean
        stats[1, m, dates] = jnp.sum(dev * dev, axis=0)

    def one_date(d, carry):
        lane = lax.broadcasted_iota(jnp.int32, (WIN, LANES), 1)
        first = lane < WIN
        near_low = lane < LANES - MARGIN
        near_high = lane < MARGIN
        present = pr_ref[d, p]
        for m in range(strips):
            rows = []
            turns = []
            for q in (2 * m, 2 * m + 1):
                start = jnp.where(
                    present != 0, p * WIN + MARGIN + at_ref[d, p, q], lines + 2 * MARGIN
                )
                rows.append(pl.ds(start, WIN))
                turns.append((LANES - ct_ref[d, p, q]) % LANES)
            part = []
            for c in range(2):
                even = wide[d, c, m, rows[0], :]
                below = wide[d, c, m - 1, rows[0], :] if m > 0 else jnp.zeros_like(even)
                odd = wide[d, c, m, rows[1], :]
                above = wide[d, c, m + 1, rows[1], :] if m + 1 < strips else jnp.zeros_like(odd)
                even = pltpu.roll(jnp.where(near_low, even, below), turns[0], 1)
                odd = pltpu.roll(jnp.where(near_high, above, odd), turns[1], 1)
                part.append(jnp.where(first, even, odd))
            sr, si = part
            amp = root(sr * sr + si * si).reshape(WIN // 8, 8, LANES)
            mean = jnp.sum(amp, axis=0) * (8.0 / WIN)
            dev = amp - mean[None]
            stats[0, m, d] = mean
            stats[1, m, d] = jnp.sum(dev * dev, axis=0)
            stats[2, m, d] = jnp.sum(dev * band[2, m].reshape(WIN // 8, 8, LANES), axis=0)
            rr = band[0, m]
            ri = band[1, m]
            for c, value in enumerate((rr * sr + ri * si, ri * sr - rr * si)):
                high, low = split(value)
                prod[d, c, :, m * LANES : (m + 1) * LANES] = high
                prod[d, c, :, (strips + m) * LANES : (strips + m + 1) * LANES] = low
        return carry

    lax.fori_loop(0, dates, one_date, 0)
    width = 2 * strips * LANES
    sums = dot(prod[...].reshape(dates * 2 * WIN, width), rgp_ref[...])
    pooled[:, :, pl.ds(pl.multiple_of(p * WIN, WIN), WIN), :] = sums.reshape(dates, 2, WIN, -1)

    half = blk_ref[0]

    def total(x):
        flat = x.reshape(-1, LANES)
        return jnp.sum(dot_right(flat, half).reshape(-1, 8, LANES), axis=1, keepdims=True)

    count = 8.0 * WIN
    means = stats[0].reshape(strips * (dates + 1), 8, LANES)
    away = means - total(means) * (1.0 / count)
    spread = stats[1].reshape(strips * (dates + 1), 8, LANES)
    var = total(spread + (WIN / 8.0) * (away * away)) * (1.0 / (WIN * WIN))
    away = away.reshape(strips, dates + 1, 8, LANES)
    var = var.reshape(strips, dates + 1, 1, LANES)
    joint = stats[2][:, :dates] + (WIN / 8.0) * (away[:, :dates] * away[:, dates:])
    cov = total(joint).reshape(strips, dates, 1, LANES) * (1.0 / (WIN * WIN))
    corr = cov / jnp.sqrt((var[:, dates:] + VAR_EPS) * (var[:, :dates] + VAR_EPS))
    lane = lax.broadcasted_iota(jnp.int32, (dates, 1, LANES), 2)
    found = jnp.zeros((dates, 1, LANES), F32)
    for m in range(strips):
        here = corr[m]
        other = pltpu.roll(here.reshape(dates, LANES), WIN, 1).reshape(dates, 1, LANES)
        left = jnp.where(lane < WIN, here, other)
        right = jnp.where(lane < WIN, other, here)
        found = jnp.where(lane == 2 * m, left, jnp.where(lane == 2 * m + 1, right, found))
    sims[p] = found


def goldstein(dates, out_ref, dft_ref, blk_ref, azp_ref, pooled):
    az_pool = azp_ref[...]
    looks_az = az_pool.shape[0]
    rows_fwd = dft_ref[0]
    cols_fwd = dft_ref[1]

    def rows_to_cols(x):
        return jnp.concatenate([x[:looks_az], x[looks_az:]], axis=1)

    turned = []
    for d in range(dates):
        z = jnp.concatenate([dot_left(az_pool, pooled[d, c]) for c in range(2)], axis=0)
        turned.append(rows_to_cols(dot_high(rows_fwd, z)))
    spectrum = dot_high(jnp.concatenate(turned, axis=0), cols_fwd)
    squares = spectrum * spectrum
    magnitude = root(squares + pltpu.roll(squares, WIN, 1))
    smooth = dot_right(magnitude, blk_ref[1]).reshape(-1, PATCH, LANES)
    smooth = (
        smooth
        + jnp.concatenate([smooth[:, 1:], smooth[:, :1]], axis=1)
        + jnp.concatenate([smooth[:, -1:], smooth[:, :-1]], axis=1)
    ).reshape(spectrum.shape)
    weighted = spectrum * root(smooth * (1.0 / 9.0))
    turned = []
    for d in range(dates):
        w = weighted[d * looks_az : (d + 1) * looks_az]
        w = jnp.concatenate([w[:, :WIN], w[:, WIN:]], axis=0)
        turned.append(rows_to_cols(dot_high(cols_fwd, w)))
    back = dot_high(jnp.concatenate(turned, axis=0), rows_fwd)
    squares = back * back
    power = dot_right(squares + pltpu.roll(squares, WIN, 1), blk_ref[2]).reshape(-1, PATCH, LANES)
    power = jnp.sum(power, axis=1, keepdims=True) * (1.0 / (PATCH * PATCH))
    scaled = back.reshape(-1, PATCH, LANES) * lax.rsqrt(power + RMS_EPS)
    scaled = scaled.reshape(back.shape)
    for d in range(dates):
        rows = scaled[d * looks_az : (d + 1) * looks_az]
        out_ref[d, 0] = rows[:, :WIN]
        out_ref[d, 1] = rows[:, WIN:]


def kernel(
    at_ref, ct_ref, pr_ref, img_ref, low_ref, high_ref, ref_ref, dft_ref, blk_ref, azp_ref, rgp_ref,
    sim_ref, out_ref,
    wide, band, prod, pooled, stats, sims,
):
    dates, _, lines, samples = img_ref.shape
    strips = samples // LANES
    rows = lines // WIN

    def widen(i, carry):
        d = i // 2
        c = i % 2
        for m in range(strips):
            cols = slice(m * LANES, (m + 1) * LANES)
            wide[d, c, m, 0:MARGIN, :] = low_ref[d, c, :, cols].astype(F32)
            wide[d, c, m, MARGIN : MARGIN + lines, :] = img_ref[d, c, :, cols].astype(F32)
            wide[d, c, m, MARGIN + lines : 2 * MARGIN + lines, :] = high_ref[d, c, :, cols].astype(F32)
            wide[d, c, m, 2 * MARGIN + lines : 2 * MARGIN + lines + WIN, :] = jnp.zeros((WIN, LANES), F32)
        return carry

    lax.fori_loop(0, 2 * dates, widen, 0)
    stats[2] = jnp.zeros(stats.shape[1:], F32)

    def row(p, carry):
        def ref_chunk(c, cols):
            return ref_ref[c, pl.ds(pl.multiple_of(p * WIN, WIN), WIN), cols].astype(F32)

        window_row(
            p, (dates, lines, strips), at_ref, ct_ref, pr_ref, ref_chunk, blk_ref, rgp_ref,
            wide, band, prod, pooled, stats, sims,
        )
        return carry

    lax.fori_loop(0, rows, row, 0)
    for p in range(rows):
        sim_ref[:, p : p + 1, :] = sims[p][:, :, : sim_ref.shape[2]]
    goldstein(dates, out_ref, dft_ref, blk_ref, azp_ref, pooled)


def broadcast(x, axis, root_index):
    mine = lax.axis_index(axis) == root_index
    return lax.psum(jnp.where(mine, x, jnp.zeros_like(x)), axis)


def on_device(image, along, cross, present):
    dates, _, lines, samples = image.shape
    strips = samples // LANES
    rows = lines // WIN
    ref = broadcast(image[0], "date", 0)
    count = lax.axis_size("az")
    forward = [(i, i + 1) for i in range(count - 1)]
    backward = [(b, a) for a, b in forward]
    low = lax.ppermute(image[:, :, lines - MARGIN :], "az", forward)
    high = lax.ppermute(image[:, :, :MARGIN], "az", backward)
    smem = pl.BlockSpec(memory_space=pltpu.SMEM)
    vmem = pl.BlockSpec(memory_space=pltpu.VMEM)
    return pl.pallas_call(
        kernel,
        out_shape=(
            jax.ShapeDtypeStruct((dates, rows, samples // WIN), F32),
            jax.ShapeDtypeStruct((dates, 2, lines // LOOK_AZ, samples // LOOK_RG), F32),
        ),
        in_specs=[smem] * 3 + [vmem] * 8,
        out_specs=(vmem, vmem),
        scratch_shapes=[
            pltpu.VMEM((dates, 2, strips, lines + 2 * MARGIN + WIN, LANES), F32),
            pltpu.VMEM((3, strips, WIN, LANES), F32),
            pltpu.VMEM((dates, 2, WIN, 2 * samples), BF16),
            pltpu.VMEM((dates, 2, lines, samples // LOOK_RG), F32),
            pltpu.VMEM((3, strips, dates + 1, 8, LANES), F32),
            pltpu.VMEM((rows, dates, 1, LANES), F32),
        ],
        compiler_params=pltpu.CompilerParams(vmem_limit_bytes=56 * 1024 * 1024),
    )(along, cross, present, image, low, high, ref, *tables(lines, samples))


def solution(mesh):
    placed = (
        P("date", None, "az", None),
        P("date", "az", None),
        P("date", "az", None),
        P("date", "az"),
    )
    return jax.shard_map(
        on_device,
        mesh=mesh,
        in_specs=placed,
        out_specs=(P("date", "az", None), P("date", None, "az", None)),
        check_vma=False,
    )
```

```python
import jax
import jax.numpy as jnp
import numpy as np
from jax import lax
from jax.experimental import pallas as pl
from jax.experimental.pallas import tpu as pltpu
from jax.sharding import PartitionSpec as P

WIN = 64
MARGIN = 32
LOOK_AZ = 5
LOOK_RG = 20
PATCH = 32
LANES = 128
PIECE = 16
AHEAD = 8

VAR_EPS = 1e-05
RMS_EPS = 1e-06
TINY = 1e-37

F32 = jnp.float32
BF16 = jnp.bfloat16


def tables(lines, samples):
    turns = np.outer(np.arange(PATCH), np.arange(PATCH)) % PATCH
    angles = turns * (2.0 * np.pi / PATCH)
    two = np.eye(2)
    cosine = np.kron(two, np.cos(angles))
    sine = np.kron(two, np.sin(angles))
    rows_fwd = np.block([[cosine, sine], [-sine, cosine]])
    cols_fwd = np.block([[cosine, -sine], [sine, cosine]])
    dft = np.stack([rows_fwd, cols_fwd]).astype(np.float32)
    near = np.abs(np.arange(PATCH)[:, None] - np.arange(PATCH)[None, :])
    circular = np.minimum(near, PATCH - near) <= 1
    four = np.eye(LANES // PATCH)
    half = np.kron(np.eye(2), np.ones((WIN, WIN)))
    blocks = np.stack(
        [half, np.kron(four, circular), np.kron(four, np.ones((PATCH, PATCH)))]
    ).astype(np.float32)
    az_pool = (
        np.arange(lines // LOOK_AZ)[:, None] == np.arange(lines)[None, :] // LOOK_AZ
    ).astype(np.float32)
    rg_pool = (
        np.arange(samples)[:, None] // LOOK_RG == np.arange(samples // LOOK_RG)[None, :]
    ).astype(np.float32)
    rg_pool = np.concatenate([rg_pool, rg_pool], axis=0)
    return (
        jnp.asarray(dft),
        jnp.asarray(blocks, BF16),
        jnp.asarray(az_pool, BF16),
        jnp.asarray(rg_pool, BF16),
    )


def dot(a, b):
    return jnp.dot(a, b, preferred_element_type=F32)


def dot_high(a, b):
    return jnp.dot(a, b, preferred_element_type=F32, precision=lax.Precision.HIGHEST)


def split(x):
    high = x.astype(BF16)
    return high, (x - high.astype(F32)).astype(BF16)


def dot_right(x, ones):
    high, low = split(x)
    return dot(high, ones) + dot(low, ones)


def dot_left(ones, x):
    high, low = split(x)
    return dot(ones, high) + dot(ones, low)


def root(x):
    return x * lax.rsqrt(jnp.maximum(x, TINY))


def window_row(p, sizes, at_ref, ct_ref, pr_ref, ref_chunk, blk_ref, rgp_ref, wide, band, prod, pooled, stats, sims, follow):
    dates, lines, strips = sizes
    for m in range(strips):
        cols = slice(m * LANES, (m + 1) * LANES)
        real = ref_chunk(0, cols)
        imag = ref_chunk(1, cols)
        band[0, m] = real
        band[1, m] = imag
        amp = root(real * real + imag * imag).reshape(WIN // 8, 8, LANES)
        mean = jnp.sum(amp, axis=0) * (8.0 / WIN)
        dev = amp - mean[None]
        band[2, m] = dev.reshape(WIN, LANES)
        stats[0, m, dates] = mean
        stats[1, m, dates] = jnp.sum(dev * dev, axis=0)

    def one_date(d, carry):
        follow(d)
        lane = lax.broadcasted_iota(jnp.int32, (WIN, LANES), 1)
        first = lane < WIN
        near_low = lane < LANES - MARGIN
        near_high = lane < MARGIN
        present = pr_ref[d, p]
        for m in range(strips):
            rows = []
            turns = []
            for q in (2 * m, 2 * m + 1):
                start = jnp.where(
                    present != 0, p * WIN + MARGIN + at_ref[d, p, q], lines + 2 * MARGIN
                )
                rows.append(pl.ds(start, WIN))
                turns.append((LANES - ct_ref[d, p, q]) % LANES)
            part = []
            for c in range(2):
                even = wide[d, c, m, rows[0], :]
                below = wide[d, c, m - 1, rows[0], :] if m > 0 else jnp.zeros_like(even)
                odd = wide[d, c, m, rows[1], :]
                above = wide[d, c, m + 1, rows[1], :] if m + 1 < strips else jnp.zeros_like(odd)
                even = pltpu.roll(jnp.where(near_low, even, below), turns[0], 1)
                odd = pltpu.roll(jnp.where(near_high, above, odd), turns[1], 1)
                part.append(jnp.where(first, even, odd))
            sr, si = part
            amp = root(sr * sr + si * si).reshape(WIN // 8, 8, LANES)
            mean = jnp.sum(amp, axis=0) * (8.0 / WIN)
            dev = amp - mean[None]
            stats[0, m, d] = mean
            stats[1, m, d] = jnp.sum(dev * dev, axis=0)
            stats[2, m, d] = jnp.sum(dev * band[2, m].reshape(WIN // 8, 8, LANES), axis=0)
            rr = band[0, m]
            ri = band[1, m]
            for c, value in enumerate((rr * sr + ri * si, ri * sr - rr * si)):
                high, low = split(value)
                prod[d, c, :, m * LANES : (m + 1) * LANES] = high
                prod[d, c, :, (strips + m) * LANES : (strips + m + 1) * LANES] = low
        return carry

    lax.fori_loop(0, dates, one_date, 0)
    width = 2 * strips * LANES
    sums = dot(prod[...].reshape(dates * 2 * WIN, width), rgp_ref[...])
    pooled[:, :, pl.ds(pl.multiple_of(p * WIN, WIN), WIN), :] = sums.reshape(dates, 2, WIN, -1)

    half = blk_ref[0]

    def total(x):
        flat = x.reshape(-1, LANES)
        return jnp.sum(dot_right(flat, half).reshape(-1, 8, LANES), axis=1, keepdims=True)

    count = 8.0 * WIN
    means = stats[0].reshape(strips * (dates + 1), 8, LANES)
    away = means - total(means) * (1.0 / count)
    spread = stats[1].reshape(strips * (dates + 1), 8, LANES)
    var = total(spread + (WIN / 8.0) * (away * away)) * (1.0 / (WIN * WIN))
    away = away.reshape(strips, dates + 1, 8, LANES)
    var = var.reshape(strips, dates + 1, 1, LANES)
    joint = stats[2][:, :dates] + (WIN / 8.0) * (away[:, :dates] * away[:, dates:])
    cov = total(joint).reshape(strips, dates, 1, LANES) * (1.0 / (WIN * WIN))
    corr = cov / jnp.sqrt((var[:, dates:] + VAR_EPS) * (var[:, :dates] + VAR_EPS))
    lane = lax.broadcasted_iota(jnp.int32, (dates, 1, LANES), 2)
    found = jnp.zeros((dates, 1, LANES), F32)
    for m in range(strips):
        here = corr[m]
        other = pltpu.roll(here.reshape(dates, LANES), WIN, 1).reshape(dates, 1, LANES)
        left = jnp.where(lane < WIN, here, other)
        right = jnp.where(lane < WIN, other, here)
        found = jnp.where(lane == 2 * m, left, jnp.where(lane == 2 * m + 1, right, found))
    sims[p] = found


def goldstein(dates, out_ref, dft_ref, blk_ref, azp_ref, pooled):
    az_pool = azp_ref[...]
    looks_az = az_pool.shape[0]
    rows_fwd = dft_ref[0]
    cols_fwd = dft_ref[1]

    def rows_to_cols(x):
        return jnp.concatenate([x[:looks_az], x[looks_az:]], axis=1)

    turned = []
    for d in range(dates):
        z = jnp.concatenate([dot_left(az_pool, pooled[d, c]) for c in range(2)], axis=0)
        turned.append(rows_to_cols(dot_high(rows_fwd, z)))
    spectrum = dot_high(jnp.concatenate(turned, axis=0), cols_fwd)
    squares = spectrum * spectrum
    magnitude = root(squares + pltpu.roll(squares, WIN, 1))
    smooth = dot_right(magnitude, blk_ref[1]).reshape(-1, PATCH, LANES)
    smooth = (
        smooth
        + jnp.concatenate([smooth[:, 1:], smooth[:, :1]], axis=1)
        + jnp.concatenate([smooth[:, -1:], smooth[:, :-1]], axis=1)
    ).reshape(spectrum.shape)
    weighted = spectrum * root(smooth * (1.0 / 9.0))
    turned = []
    for d in range(dates):
        w = weighted[d * looks_az : (d + 1) * looks_az]
        w = jnp.concatenate([w[:, :WIN], w[:, WIN:]], axis=0)
        turned.append(rows_to_cols(dot_high(cols_fwd, w)))
    back = dot_high(jnp.concatenate(turned, axis=0), rows_fwd)
    squares = back * back
    power = dot_right(squares + pltpu.roll(squares, WIN, 1), blk_ref[2]).reshape(-1, PATCH, LANES)
    power = jnp.sum(power, axis=1, keepdims=True) * (1.0 / (PATCH * PATCH))
    scaled = back.reshape(-1, PATCH, LANES) * lax.rsqrt(power + RMS_EPS)
    scaled = scaled.reshape(back.shape)
    for d in range(dates):
        rows = scaled[d * looks_az : (d + 1) * looks_az]
        out_ref[d, 0] = rows[:, :WIN]
        out_ref[d, 1] = rows[:, WIN:]


def ring_device(position, count):
    half = count // 2
    return jnp.where(position < half, 2 * position, 2 * (count - 1 - position) + 1)


def kernel(
    at_ref, ct_ref, pr_ref, img_ref, dft_ref, blk_ref, azp_ref, rgp_ref,
    sim_ref, out_ref,
    image, halo, ref, wide, band, prod, pooled, stats, sims,
    image_sem, root_sem, halo_send, halo_recv, ref_send, ref_recv,
):
    dates, _, lines, samples = img_ref.shape
    strips = samples // LANES
    rows = lines // WIN
    pieces = ref_send.shape[1]
    height = lines // pieces
    each = WIN // height
    count = lax.axis_size("date")
    az_count = lax.axis_size("az")
    az = lax.axis_index("az")
    mine = lax.axis_index("date")
    position = jnp.where(mine % 2 == 0, mine // 2, count - 1 - mine // 2)
    after = ring_device((position + 1) % count, count)
    before = ring_device((position + count - 1) % count, count)
    hops = (position, (count - position) % count)
    targets = (after, before)
    mesh_ids = pl.DeviceIdType.MESH

    def load(i):
        d = i // 2
        c = i % 2
        return pltpu.make_async_copy(img_ref.at[d, c], image.at[d, c], image_sem.at[i])

    for i in range(2 * dates):
        load(i).start()
    own = pltpu.make_async_copy(img_ref.at[0], ref, root_sem)

    @pl.when(mine == 0)
    def _():
        own.start()

    barrier = pltpu.get_barrier_semaphore()
    for target in targets:
        pl.semaphore_signal(barrier, inc=1, device_id={"date": target}, device_id_type=mesh_ids)

    @pl.when(az > 0)
    def _():
        pl.semaphore_signal(barrier, inc=1, device_id={"az": az - 1}, device_id_type=mesh_ids)

    @pl.when(az < az_count - 1)
    def _():
        pl.semaphore_signal(barrier, inc=1, device_id={"az": az + 1}, device_id_type=mesh_ids)

    peers = 2 + jnp.where(az > 0, 1, 0) + jnp.where(az < az_count - 1, 1, 0)
    pl.semaphore_wait(barrier, peers)

    def row_of(s):
        return jnp.where(s < rows - 2, s + 1, jnp.where(s == rows - 2, 0, rows - 1))

    def piece_rows(j):
        return pl.ds(pl.multiple_of(row_of(j // each) * WIN + (j % each) * height, height), height)

    def relay(c, j, first):
        at = piece_rows(j)
        return pltpu.make_async_remote_copy(
            src_ref=img_ref.at[0, c, at] if first else ref.at[c, at],
            dst_ref=ref.at[c, at],
            send_sem=ref_send.at[c, j],
            recv_sem=ref_recv.at[c, j],
            device_id={"date": targets[c]},
            device_id_type=mesh_ids,
        )

    def launch(j):
        for c in range(2):
            relay(c, j, True).start()

    def pass_on(j):
        for c in range(2):
            @pl.when(hops[c] > 0)
            def _():
                relay(c, j, False).wait_recv()

            @pl.when((hops[c] > 0) & (hops[c] < count - 1))
            def _():
                relay(c, j, False).start()

        @pl.when((mine == 0) & (j + AHEAD < pieces))
        def _():
            launch(j + AHEAD)

    @pl.when(mine == 0)
    def _():
        for j in range(AHEAD):
            launch(j)

    def edge(k):
        start = 0 if k else lines - MARGIN
        return pltpu.make_async_remote_copy(
            src_ref=img_ref.at[:, :, pl.ds(start, MARGIN)],
            dst_ref=halo.at[k],
            send_sem=halo_send.at[k],
            recv_sem=halo_recv.at[k],
            device_id={"az": az - 1 if k else az + 1},
            device_id_type=mesh_ids,
        )

    sends = (az < az_count - 1, az > 0)
    takes = (az > 0, az < az_count - 1)
    for k in range(2):
        @pl.when(sends[k])
        def _():
            edge(k).start()

    def widen(i, carry):
        d = i // 2
        c = i % 2
        load(i).wait()
        for m in range(strips):
            cols = slice(m * LANES, (m + 1) * LANES)
            wide[d, c, m, MARGIN : MARGIN + lines, :] = image[d, c, :, cols].astype(F32)
            wide[d, c, m, 2 * MARGIN + lines : 2 * MARGIN + lines + WIN, :] = jnp.zeros((WIN, LANES), F32)

        @pl.when(i >= 2 * dates - each)
        def _():
            pass_on(i - (2 * dates - each))

        return carry

    lax.fori_loop(0, 2 * dates, widen, 0)

    @pl.when(mine == 0)
    def _():
        own.wait()

    stats[2] = jnp.zeros(stats.shape[1:], F32)

    def fringe(k):
        first = MARGIN + lines if k else 0

        @pl.when(takes[k])
        def _():
            edge(k).wait_recv()

            def convert(i, carry):
                d = i // 2
                c = i % 2
                for m in range(strips):
                    cols = slice(m * LANES, (m + 1) * LANES)
                    wide[d, c, m, first : first + MARGIN, :] = halo[k, d, c, :, cols].astype(F32)
                return carry

            lax.fori_loop(0, 2 * dates, convert, 0)

        @pl.when(jnp.logical_not(takes[k]))
        def _():
            def clear(i, carry):
                for m in range(strips):
                    wide[i // 2, i % 2, m, first : first + MARGIN, :] = jnp.zeros((MARGIN, LANES), F32)
                return carry

            lax.fori_loop(0, 2 * dates, clear, 0)

    def row(s, carry):
        @pl.when(s == rows - 2)
        def _():
            for k in range(2):
                fringe(k)

        p = row_of(s)

        def ref_chunk(c, cols):
            return ref[c, pl.ds(pl.multiple_of(p * WIN, WIN), WIN), cols].astype(F32)

        def follow(d):
            for e in range(each // dates if each >= dates else 1):
                j = (s + 1) * each + d * max(each // dates, 1) + e

                @pl.when((s < rows - 1) & (j < (s + 2) * each))
                def _():
                    pass_on(j)

        window_row(
            p, (dates, lines, strips), at_ref, ct_ref, pr_ref, ref_chunk, blk_ref, rgp_ref,
            wide, band, prod, pooled, stats, sims, follow,
        )
        return carry

    lax.fori_loop(0, rows, row, 0)
    for p in range(rows):
        sim_ref[:, p : p + 1, :] = sims[p][:, :, : sim_ref.shape[2]]
    goldstein(dates, out_ref, dft_ref, blk_ref, azp_ref, pooled)

    for c in range(2):
        @pl.when(hops[c] < count - 1)
        def _():
            def drain(j, carry):
                relay(c, j, False).wait_send()
                return carry

            lax.fori_loop(0, pieces, drain, 0)

    for k in range(2):
        @pl.when(sends[k])
        def _():
            edge(k).wait_send()


def on_device(image, along, cross, present):
    dates, _, lines, samples = image.shape
    strips = samples // LANES
    rows = lines // WIN
    pieces = lines // PIECE
    smem = pl.BlockSpec(memory_space=pltpu.SMEM)
    vmem = pl.BlockSpec(memory_space=pltpu.VMEM)
    dma = pltpu.SemaphoreType.DMA
    return pl.pallas_call(
        kernel,
        out_shape=(
            jax.ShapeDtypeStruct((dates, rows, samples // WIN), F32),
            jax.ShapeDtypeStruct((dates, 2, lines // LOOK_AZ, samples // LOOK_RG), F32),
        ),
        in_specs=[smem] * 3 + [pl.BlockSpec(memory_space=pl.ANY)] + [vmem] * 4,
        out_specs=(vmem, vmem),
        scratch_shapes=[
            pltpu.VMEM((dates, 2, lines, samples), BF16),
            pltpu.VMEM((2, dates, 2, MARGIN, samples), BF16),
            pltpu.VMEM((2, lines, samples), BF16),
            pltpu.VMEM((dates, 2, strips, lines + 2 * MARGIN + WIN, LANES), F32),
            pltpu.VMEM((3, strips, WIN, LANES), F32),
            pltpu.VMEM((dates, 2, WIN, 2 * samples), BF16),
            pltpu.VMEM((dates, 2, lines, samples // LOOK_RG), F32),
            pltpu.VMEM((3, strips, dates + 1, 8, LANES), F32),
            pltpu.VMEM((rows, dates, 1, LANES), F32),
            dma((2 * dates,)),
            dma(()),
            dma((2,)),
            dma((2,)),
            dma((2, pieces)),
            dma((2, pieces)),
        ],
        compiler_params=pltpu.CompilerParams(
            vmem_limit_bytes=56 * 1024 * 1024, collective_id=0, has_side_effects=True
        ),
    )(along, cross, present, image, *tables(lines, samples))


def solution(mesh):
    placed = (
        P("date", None, "az", None),
        P("date", "az", None),
        P("date", "az", None),
        P("date", "az"),
    )
    return jax.shard_map(
        on_device,
        mesh=mesh,
        in_specs=placed,
        out_specs=(P("date", "az", None), P("date", None, "az", None)),
        check_vma=False,
    )
```

```python
import jax
import jax.numpy as jnp
import numpy as np
from jax import lax
from jax.experimental import pallas as pl
from jax.experimental.pallas import tpu as pltpu
from jax.sharding import PartitionSpec as P

WIN = 64
MARGIN = 32
LOOK_AZ = 5
LOOK_RG = 20
PATCH = 32
LANES = 128
PIECE = 16
AHEAD = 8
LAG = 3

VAR_EPS = 1e-05
RMS_EPS = 1e-06
TINY = 1e-37

F32 = jnp.float32
BF16 = jnp.bfloat16


def tables(lines, samples):
    turns = np.outer(np.arange(PATCH), np.arange(PATCH)) % PATCH
    angles = turns * (2.0 * np.pi / PATCH)
    two = np.eye(2)
    cosine = np.kron(two, np.cos(angles))
    sine = np.kron(two, np.sin(angles))
    rows_fwd = np.block([[cosine, sine], [-sine, cosine]])
    cols_fwd = np.block([[cosine, -sine], [sine, cosine]])
    dft = np.stack([rows_fwd, cols_fwd]).astype(np.float32)
    near = np.abs(np.arange(PATCH)[:, None] - np.arange(PATCH)[None, :])
    circular = np.minimum(near, PATCH - near) <= 1
    four = np.eye(LANES // PATCH)
    half = np.kron(np.eye(2), np.ones((WIN, WIN)))
    blocks = np.stack(
        [half, np.kron(four, circular), np.kron(four, np.ones((PATCH, PATCH)))]
    ).astype(np.float32)
    az_pool = (
        np.arange(lines // LOOK_AZ)[:, None] == np.arange(lines)[None, :] // LOOK_AZ
    ).astype(np.float32)
    rg_pool = (
        np.arange(samples)[:, None] // LOOK_RG == np.arange(samples // LOOK_RG)[None, :]
    ).astype(np.float32)
    rg_pool = np.concatenate([rg_pool, rg_pool], axis=0)
    return (
        jnp.asarray(dft),
        jnp.asarray(blocks, BF16),
        jnp.asarray(az_pool, BF16),
        jnp.asarray(rg_pool, BF16),
    )


def dot(a, b):
    return jnp.dot(a, b, preferred_element_type=F32)


def dot_high(a, b):
    return jnp.dot(a, b, preferred_element_type=F32, precision=lax.Precision.HIGHEST)


def split(x):
    high = x.astype(BF16)
    return high, (x - high.astype(F32)).astype(BF16)


def dot_right(x, ones):
    high, low = split(x)
    return dot(high, ones) + dot(low, ones)


def dot_left(ones, x):
    high, low = split(x)
    return dot(ones, high) + dot(ones, low)


def root(x):
    return x * lax.rsqrt(jnp.maximum(x, TINY))


def window_row(p, sizes, at_ref, ct_ref, pr_ref, ref_chunk, blk_ref, rgp_ref, wide, band, prod, pooled, stats, sims, follow):
    dates, lines, strips = sizes
    for m in range(strips):
        cols = slice(m * LANES, (m + 1) * LANES)
        real = ref_chunk(0, cols)
        imag = ref_chunk(1, cols)
        band[0, m] = real
        band[1, m] = imag
        amp = root(real * real + imag * imag).reshape(WIN // 8, 8, LANES)
        mean = jnp.sum(amp, axis=0) * (8.0 / WIN)
        dev = amp - mean[None]
        band[2, m] = dev.reshape(WIN, LANES)
        stats[0, m, dates] = mean
        stats[1, m, dates] = jnp.sum(dev * dev, axis=0)

    def one_date(d, carry):
        follow(d)
        lane = lax.broadcasted_iota(jnp.int32, (WIN, LANES), 1)
        first = lane < WIN
        near_low = lane < LANES - MARGIN
        near_high = lane < MARGIN
        present = pr_ref[d, p]
        for m in range(strips):
            rows = []
            turns = []
            for q in (2 * m, 2 * m + 1):
                start = jnp.where(
                    present != 0, p * WIN + MARGIN + at_ref[d, p, q], lines + 2 * MARGIN
                )
                rows.append(pl.ds(start, WIN))
                turns.append((LANES - ct_ref[d, p, q]) % LANES)
            part = []
            for c in range(2):
                even = wide[d, c, m, rows[0], :]
                below = wide[d, c, m - 1, rows[0], :] if m > 0 else jnp.zeros_like(even)
                odd = wide[d, c, m, rows[1], :]
                above = wide[d, c, m + 1, rows[1], :] if m + 1 < strips else jnp.zeros_like(odd)
                even = pltpu.roll(jnp.where(near_low, even, below), turns[0], 1)
                odd = pltpu.roll(jnp.where(near_high, above, odd), turns[1], 1)
                part.append(jnp.where(first, even, odd))
            sr, si = part
            amp = root(sr * sr + si * si).reshape(WIN // 8, 8, LANES)
            mean = jnp.sum(amp, axis=0) * (8.0 / WIN)
            dev = amp - mean[None]
            stats[0, m, d] = mean
            stats[1, m, d] = jnp.sum(dev * dev, axis=0)
            stats[2, m, d] = jnp.sum(dev * band[2, m].reshape(WIN // 8, 8, LANES), axis=0)
            rr = band[0, m]
            ri = band[1, m]
            for c, value in enumerate((rr * sr + ri * si, ri * sr - rr * si)):
                high, low = split(value)
                prod[d, c, :, m * LANES : (m + 1) * LANES] = high
                prod[d, c, :, (strips + m) * LANES : (strips + m + 1) * LANES] = low
        return carry

    lax.fori_loop(0, dates, one_date, 0)
    width = 2 * strips * LANES
    sums = dot(prod[...].reshape(dates * 2 * WIN, width), rgp_ref[...])
    pooled[:, :, pl.ds(pl.multiple_of(p * WIN, WIN), WIN), :] = sums.reshape(dates, 2, WIN, -1)

    half = blk_ref[0]

    def total(x):
        flat = x.reshape(-1, LANES)
        return jnp.sum(dot_right(flat, half).reshape(-1, 8, LANES), axis=1, keepdims=True)

    count = 8.0 * WIN
    means = stats[0].reshape(strips * (dates + 1), 8, LANES)
    away = means - total(means) * (1.0 / count)
    spread = stats[1].reshape(strips * (dates + 1), 8, LANES)
    var = total(spread + (WIN / 8.0) * (away * away)) * (1.0 / (WIN * WIN))
    away = away.reshape(strips, dates + 1, 8, LANES)
    var = var.reshape(strips, dates + 1, 1, LANES)
    joint = stats[2][:, :dates] + (WIN / 8.0) * (away[:, :dates] * away[:, dates:])
    cov = total(joint).reshape(strips, dates, 1, LANES) * (1.0 / (WIN * WIN))
    corr = cov / jnp.sqrt((var[:, dates:] + VAR_EPS) * (var[:, :dates] + VAR_EPS))
    lane = lax.broadcasted_iota(jnp.int32, (dates, 1, LANES), 2)
    found = jnp.zeros((dates, 1, LANES), F32)
    for m in range(strips):
        here = corr[m]
        other = pltpu.roll(here.reshape(dates, LANES), WIN, 1).reshape(dates, 1, LANES)
        left = jnp.where(lane < WIN, here, other)
        right = jnp.where(lane < WIN, other, here)
        found = jnp.where(lane == 2 * m, left, jnp.where(lane == 2 * m + 1, right, found))
    sims[p] = found


def goldstein(dates, out_ref, dft_ref, blk_ref, azp_ref, pooled):
    az_pool = azp_ref[...]
    looks_az = az_pool.shape[0]
    rows_fwd = dft_ref[0]
    cols_fwd = dft_ref[1]

    def rows_to_cols(x):
        return jnp.concatenate([x[:looks_az], x[looks_az:]], axis=1)

    turned = []
    for d in range(dates):
        z = jnp.concatenate([dot_left(az_pool, pooled[d, c]) for c in range(2)], axis=0)
        turned.append(rows_to_cols(dot_high(rows_fwd, z)))
    spectrum = dot_high(jnp.concatenate(turned, axis=0), cols_fwd)
    squares = spectrum * spectrum
    magnitude = root(squares + pltpu.roll(squares, WIN, 1))
    smooth = dot_right(magnitude, blk_ref[1]).reshape(-1, PATCH, LANES)
    smooth = (
        smooth
        + jnp.concatenate([smooth[:, 1:], smooth[:, :1]], axis=1)
        + jnp.concatenate([smooth[:, -1:], smooth[:, :-1]], axis=1)
    ).reshape(spectrum.shape)
    weighted = spectrum * root(smooth * (1.0 / 9.0))
    turned = []
    for d in range(dates):
        w = weighted[d * looks_az : (d + 1) * looks_az]
        w = jnp.concatenate([w[:, :WIN], w[:, WIN:]], axis=0)
        turned.append(rows_to_cols(dot_high(cols_fwd, w)))
    back = dot_high(jnp.concatenate(turned, axis=0), rows_fwd)
    squares = back * back
    power = dot_right(squares + pltpu.roll(squares, WIN, 1), blk_ref[2]).reshape(-1, PATCH, LANES)
    power = jnp.sum(power, axis=1, keepdims=True) * (1.0 / (PATCH * PATCH))
    scaled = back.reshape(-1, PATCH, LANES) * lax.rsqrt(power + RMS_EPS)
    scaled = scaled.reshape(back.shape)
    for d in range(dates):
        rows = scaled[d * looks_az : (d + 1) * looks_az]
        out_ref[d, 0] = rows[:, :WIN]
        out_ref[d, 1] = rows[:, WIN:]


def ring_device(position, count):
    half = count // 2
    return jnp.where(position < half, 2 * position, 2 * (count - 1 - position) + 1)


def kernel(
    at_ref, ct_ref, pr_ref, img_ref, dft_ref, blk_ref, azp_ref, rgp_ref,
    sim_ref, out_ref,
    image, halo, ref, wide, band, prod, pooled, stats, sims,
    image_sem, root_sem, halo_send, halo_recv, ref_send, ref_recv,
):
    dates, _, lines, samples = img_ref.shape
    strips = samples // LANES
    rows = lines // WIN
    pieces = ref_send.shape[1]
    height = lines // pieces
    each = WIN // height
    count = lax.axis_size("date")
    az_count = lax.axis_size("az")
    az = lax.axis_index("az")
    mine = lax.axis_index("date")
    position = jnp.where(mine % 2 == 0, mine // 2, count - 1 - mine // 2)
    after = ring_device((position + 1) % count, count)
    before = ring_device((position + count - 1) % count, count)
    hops = (position, (count - position) % count)
    targets = (after, before)
    mesh_ids = pl.DeviceIdType.MESH

    def load(i):
        d = i // 2
        c = i % 2
        return pltpu.make_async_copy(img_ref.at[d, c], image.at[d, c], image_sem.at[i])

    for i in range(2 * dates):
        load(i).start()
    own = pltpu.make_async_copy(img_ref.at[0], ref, root_sem)

    @pl.when(mine == 0)
    def _():
        own.start()

    barrier = pltpu.get_barrier_semaphore()
    for target in targets:
        pl.semaphore_signal(barrier, inc=1, device_id={"date": target}, device_id_type=mesh_ids)

    @pl.when(az > 0)
    def _():
        pl.semaphore_signal(barrier, inc=1, device_id={"az": az - 1}, device_id_type=mesh_ids)

    @pl.when(az < az_count - 1)
    def _():
        pl.semaphore_signal(barrier, inc=1, device_id={"az": az + 1}, device_id_type=mesh_ids)

    peers = 2 + jnp.where(az > 0, 1, 0) + jnp.where(az < az_count - 1, 1, 0)
    pl.semaphore_wait(barrier, peers)

    def row_of(s):
        return jnp.where(s < rows - 2, s + 1, jnp.where(s == rows - 2, 0, rows - 1))

    def piece_rows(j):
        return pl.ds(pl.multiple_of(row_of(j // each) * WIN + (j % each) * height, height), height)

    def relay(c, j, first):
        at = piece_rows(j)
        return pltpu.make_async_remote_copy(
            src_ref=img_ref.at[0, c, at] if first else ref.at[c, at],
            dst_ref=ref.at[c, at],
            send_sem=ref_send.at[c, j],
            recv_sem=ref_recv.at[c, j],
            device_id={"date": targets[c]},
            device_id_type=mesh_ids,
        )

    def launch(j):
        for c in range(2):
            relay(c, j, True).start()

    def slot(t):
        for c in range(2):
            j = t - (hops[c] - 1) * LAG
            here = (hops[c] > 0) & (j >= 0) & (j < pieces)

            @pl.when(here)
            def _():
                relay(c, j, False).wait_recv()

            @pl.when(here & (hops[c] < count - 1))
            def _():
                relay(c, j, False).start()

        @pl.when((mine == 0) & (t + AHEAD < pieces))
        def _():
            launch(t + AHEAD)

    @pl.when(mine == 0)
    def _():
        for j in range(AHEAD):
            launch(j)

    def edge(k):
        start = 0 if k else lines - MARGIN
        return pltpu.make_async_remote_copy(
            src_ref=img_ref.at[:, :, pl.ds(start, MARGIN)],
            dst_ref=halo.at[k],
            send_sem=halo_send.at[k],
            recv_sem=halo_recv.at[k],
            device_id={"az": az - 1 if k else az + 1},
            device_id_type=mesh_ids,
        )

    sends = (az < az_count - 1, az > 0)
    takes = (az > 0, az < az_count - 1)
    for k in range(2):
        @pl.when(sends[k])
        def _():
            edge(k).start()

    def widen(i, carry):
        d = i // 2
        c = i % 2
        load(i).wait()
        for m in range(strips):
            cols = slice(m * LANES, (m + 1) * LANES)
            wide[d, c, m, MARGIN : MARGIN + lines, :] = image[d, c, :, cols].astype(F32)
            wide[d, c, m, 2 * MARGIN + lines : 2 * MARGIN + lines + WIN, :] = jnp.zeros((WIN, LANES), F32)

        @pl.when(i < early)
        def _():
            slot(i)

        return carry

    early = each + (count - 2) * LAG
    lax.fori_loop(0, 2 * dates, widen, 0)

    def catch_up(t, carry):
        slot(t)
        return carry

    lax.fori_loop(2 * dates, max(2 * dates, early), catch_up, 0)

    @pl.when(mine == 0)
    def _():
        own.wait()

    stats[2] = jnp.zeros(stats.shape[1:], F32)

    def fringe(k):
        first = MARGIN + lines if k else 0

        @pl.when(takes[k])
        def _():
            edge(k).wait_recv()

            def convert(i, carry):
                d = i // 2
                c = i % 2
                for m in range(strips):
                    cols = slice(m * LANES, (m + 1) * LANES)
                    wide[d, c, m, first : first + MARGIN, :] = halo[k, d, c, :, cols].astype(F32)
                return carry

            lax.fori_loop(0, 2 * dates, convert, 0)

        @pl.when(jnp.logical_not(takes[k]))
        def _():
            def clear(i, carry):
                for m in range(strips):
                    wide[i // 2, i % 2, m, first : first + MARGIN, :] = jnp.zeros((MARGIN, LANES), F32)
                return carry

            lax.fori_loop(0, 2 * dates, clear, 0)

    def row(s, carry):
        @pl.when(s == rows - 2)
        def _():
            for k in range(2):
                fringe(k)

        p = row_of(s)

        def ref_chunk(c, cols):
            return ref[c, pl.ds(pl.multiple_of(p * WIN, WIN), WIN), cols].astype(F32)

        def follow(d):
            share = -(-each // dates)
            for e in range(share):
                k = d * share + e

                @pl.when((s < rows - 1) & (k < each))
                def _():
                    slot(early + s * each + k)

        window_row(
            p, (dates, lines, strips), at_ref, ct_ref, pr_ref, ref_chunk, blk_ref, rgp_ref,
            wide, band, prod, pooled, stats, sims, follow,
        )
        return carry

    lax.fori_loop(0, rows, row, 0)
    for p in range(rows):
        sim_ref[:, p : p + 1, :] = sims[p][:, :, : sim_ref.shape[2]]
    goldstein(dates, out_ref, dft_ref, blk_ref, azp_ref, pooled)

    for c in range(2):
        @pl.when(hops[c] < count - 1)
        def _():
            def drain(j, carry):
                relay(c, j, False).wait_send()
                return carry

            lax.fori_loop(0, pieces, drain, 0)

    for k in range(2):
        @pl.when(sends[k])
        def _():
            edge(k).wait_send()


def on_device(image, along, cross, present):
    dates, _, lines, samples = image.shape
    strips = samples // LANES
    rows = lines // WIN
    pieces = lines // PIECE
    smem = pl.BlockSpec(memory_space=pltpu.SMEM)
    vmem = pl.BlockSpec(memory_space=pltpu.VMEM)
    dma = pltpu.SemaphoreType.DMA
    return pl.pallas_call(
        kernel,
        out_shape=(
            jax.ShapeDtypeStruct((dates, rows, samples // WIN), F32),
            jax.ShapeDtypeStruct((dates, 2, lines // LOOK_AZ, samples // LOOK_RG), F32),
        ),
        in_specs=[smem] * 3 + [pl.BlockSpec(memory_space=pl.ANY)] + [vmem] * 4,
        out_specs=(vmem, vmem),
        scratch_shapes=[
            pltpu.VMEM((dates, 2, lines, samples), BF16),
            pltpu.VMEM((2, dates, 2, MARGIN, samples), BF16),
            pltpu.VMEM((2, lines, samples), BF16),
            pltpu.VMEM((dates, 2, strips, lines + 2 * MARGIN + WIN, LANES), F32),
            pltpu.VMEM((3, strips, WIN, LANES), F32),
            pltpu.VMEM((dates, 2, WIN, 2 * samples), BF16),
            pltpu.VMEM((dates, 2, lines, samples // LOOK_RG), F32),
            pltpu.VMEM((3, strips, dates + 1, 8, LANES), F32),
            pltpu.VMEM((rows, dates, 1, LANES), F32),
            dma((2 * dates,)),
            dma(()),
            dma((2,)),
            dma((2,)),
            dma((2, pieces)),
            dma((2, pieces)),
        ],
        compiler_params=pltpu.CompilerParams(
            vmem_limit_bytes=56 * 1024 * 1024, collective_id=0, has_side_effects=True
        ),
    )(along, cross, present, image, *tables(lines, samples))


def solution(mesh):
    placed = (
        P("date", None, "az", None),
        P("date", "az", None),
        P("date", "az", None),
        P("date", "az"),
    )
    return jax.shard_map(
        on_device,
        mesh=mesh,
        in_specs=placed,
        out_specs=(P("date", "az", None), P("date", None, "az", None)),
        check_vma=False,
    )
```

```python
import jax
import jax.numpy as jnp
import numpy as np
from jax import lax
from jax.experimental import pallas as pl
from jax.experimental.pallas import tpu as pltpu
from jax.sharding import PartitionSpec as P

WIN = 64
MARGIN = 32
LOOK_AZ = 5
LOOK_RG = 20
PATCH = 32
LANES = 128
PIECE = 16
AHEAD = 8
LAG = 5
OPENING = 4

VAR_EPS = 1e-05
RMS_EPS = 1e-06
TINY = 1e-37

F32 = jnp.float32
BF16 = jnp.bfloat16


def tables(lines, samples):
    turns = np.outer(np.arange(PATCH), np.arange(PATCH)) % PATCH
    angles = turns * (2.0 * np.pi / PATCH)
    two = np.eye(2)
    cosine = np.kron(two, np.cos(angles))
    sine = np.kron(two, np.sin(angles))
    rows_fwd = np.block([[cosine, sine], [-sine, cosine]])
    cols_fwd = np.block([[cosine, -sine], [sine, cosine]])
    dft = np.stack([rows_fwd, cols_fwd]).astype(np.float32)
    near = np.abs(np.arange(PATCH)[:, None] - np.arange(PATCH)[None, :])
    circular = np.minimum(near, PATCH - near) <= 1
    four = np.eye(LANES // PATCH)
    half = np.kron(np.eye(2), np.ones((WIN, WIN)))
    blocks = np.stack(
        [half, np.kron(four, circular), np.kron(four, np.ones((PATCH, PATCH)))]
    ).astype(np.float32)
    az_pool = (
        np.arange(lines // LOOK_AZ)[:, None] == np.arange(lines)[None, :] // LOOK_AZ
    ).astype(np.float32)
    rg_pool = (
        np.arange(samples)[:, None] // LOOK_RG == np.arange(samples // LOOK_RG)[None, :]
    ).astype(np.float32)
    rg_pool = np.concatenate([rg_pool, rg_pool], axis=0)
    return (
        jnp.asarray(dft),
        jnp.asarray(blocks, BF16),
        jnp.asarray(az_pool, BF16),
        jnp.asarray(rg_pool, BF16),
    )


def dot(a, b):
    return jnp.dot(a, b, preferred_element_type=F32)


def dot_high(a, b):
    return jnp.dot(a, b, preferred_element_type=F32, precision=lax.Precision.HIGHEST)


def split(x):
    high = x.astype(BF16)
    return high, (x - high.astype(F32)).astype(BF16)


def dot_right(x, ones):
    high, low = split(x)
    return dot(high, ones) + dot(low, ones)


def dot_left(ones, x):
    high, low = split(x)
    return dot(ones, high) + dot(ones, low)


def root(x):
    return x * lax.rsqrt(jnp.maximum(x, TINY))


def resample(p, d, sizes, at_ref, ct_ref, pr_ref, wide, shifted, devs, stats):
    dates, lines, strips = sizes
    lane = lax.broadcasted_iota(jnp.int32, (WIN, LANES), 1)
    first = lane < WIN
    near_low = lane < LANES - MARGIN
    near_high = lane < MARGIN
    present = pr_ref[d, p]
    here = pl.ds(pl.multiple_of(p * WIN, WIN), WIN)
    for m in range(strips):
        rows = []
        turns = []
        for q in (2 * m, 2 * m + 1):
            start = jnp.where(
                present != 0, p * WIN + MARGIN + at_ref[p, d, q], lines + 2 * MARGIN
            )
            rows.append(pl.ds(start, WIN))
            turns.append((LANES - ct_ref[p, d, q]) % LANES)
        part = []
        for c in range(2):
            even = wide[d, c, m, rows[0], :]
            below = wide[d, c, m - 1, rows[0], :] if m > 0 else jnp.zeros_like(even)
            odd = wide[d, c, m, rows[1], :]
            above = wide[d, c, m + 1, rows[1], :] if m + 1 < strips else jnp.zeros_like(odd)
            even = pltpu.roll(jnp.where(near_low, even, below), turns[0], 1)
            odd = pltpu.roll(jnp.where(near_high, above, odd), turns[1], 1)
            part.append(jnp.where(first, even, odd))
            shifted[d, c, m, here, :] = part[c]
        amp = root(part[0] * part[0] + part[1] * part[1]).reshape(WIN // 8, 8, LANES)
        mean = jnp.sum(amp, axis=0) * (8.0 / WIN)
        dev = amp - mean[None]
        devs[d, m, here, :] = dev.reshape(WIN, LANES)
        stats[p, 0, m, d] = mean
        stats[p, 1, m, d] = jnp.sum(dev * dev, axis=0)


def window_row(p, sizes, ref_chunk, blk_ref, rgp_ref, shifted, devs, band, prod, pooled, stats, sims, follow):
    dates, lines, strips = sizes
    for m in range(strips):
        cols = slice(m * LANES, (m + 1) * LANES)
        real = ref_chunk(0, cols)
        imag = ref_chunk(1, cols)
        band[0, m] = real
        band[1, m] = imag
        amp = root(real * real + imag * imag).reshape(WIN // 8, 8, LANES)
        mean = jnp.sum(amp, axis=0) * (8.0 / WIN)
        dev = amp - mean[None]
        band[2, m] = dev.reshape(WIN, LANES)
        stats[p, 0, m, dates] = mean
        stats[p, 1, m, dates] = jnp.sum(dev * dev, axis=0)

    def one_date(d, carry):
        follow(d)
        here = pl.ds(pl.multiple_of(p * WIN, WIN), WIN)
        for m in range(strips):
            sr = shifted[d, 0, m, here, :]
            si = shifted[d, 1, m, here, :]
            joint = devs[d, m, here, :] * band[2, m]
            stats[p, 2, m, d] = jnp.sum(joint.reshape(WIN // 8, 8, LANES), axis=0)
            rr = band[0, m]
            ri = band[1, m]
            for c, value in enumerate((rr * sr + ri * si, ri * sr - rr * si)):
                high, low = split(value)
                prod[d, c, :, m * LANES : (m + 1) * LANES] = high
                prod[d, c, :, (strips + m) * LANES : (strips + m + 1) * LANES] = low
        return carry

    lax.fori_loop(0, dates, one_date, 0)
    width = 2 * strips * LANES
    sums = dot(prod[...].reshape(dates * 2 * WIN, width), rgp_ref[...])
    pooled[:, :, pl.ds(pl.multiple_of(p * WIN, WIN), WIN), :] = sums.reshape(dates, 2, WIN, -1)

    half = blk_ref[0]

    def total(x):
        flat = x.reshape(-1, LANES)
        return jnp.sum(dot_right(flat, half).reshape(-1, 8, LANES), axis=1, keepdims=True)

    count = 8.0 * WIN
    means = stats[p, 0].reshape(strips * (dates + 1), 8, LANES)
    away = means - total(means) * (1.0 / count)
    spread = stats[p, 1].reshape(strips * (dates + 1), 8, LANES)
    var = total(spread + (WIN / 8.0) * (away * away)) * (1.0 / (WIN * WIN))
    away = away.reshape(strips, dates + 1, 8, LANES)
    var = var.reshape(strips, dates + 1, 1, LANES)
    joint = stats[p, 2][:, :dates] + (WIN / 8.0) * (away[:, :dates] * away[:, dates:])
    cov = total(joint).reshape(strips, dates, 1, LANES) * (1.0 / (WIN * WIN))
    corr = cov / jnp.sqrt((var[:, dates:] + VAR_EPS) * (var[:, :dates] + VAR_EPS))
    lane = lax.broadcasted_iota(jnp.int32, (dates, 1, LANES), 2)
    found = jnp.zeros((dates, 1, LANES), F32)
    for m in range(strips):
        here = corr[m]
        other = pltpu.roll(here.reshape(dates, LANES), WIN, 1).reshape(dates, 1, LANES)
        left = jnp.where(lane < WIN, here, other)
        right = jnp.where(lane < WIN, other, here)
        found = jnp.where(lane == 2 * m, left, jnp.where(lane == 2 * m + 1, right, found))
    sims[p] = found


def goldstein(dates, out_ref, dft_ref, blk_ref, azp_ref, pooled):
    az_pool = azp_ref[...]
    looks_az = az_pool.shape[0]
    rows_fwd = dft_ref[0]
    cols_fwd = dft_ref[1]

    def rows_to_cols(x):
        return jnp.concatenate([x[:looks_az], x[looks_az:]], axis=1)

    turned = []
    for d in range(dates):
        z = jnp.concatenate([dot_left(az_pool, pooled[d, c]) for c in range(2)], axis=0)
        turned.append(rows_to_cols(dot_high(rows_fwd, z)))
    spectrum = dot_high(jnp.concatenate(turned, axis=0), cols_fwd)
    squares = spectrum * spectrum
    magnitude = root(squares + pltpu.roll(squares, WIN, 1))
    smooth = dot_right(magnitude, blk_ref[1]).reshape(-1, PATCH, LANES)
    smooth = (
        smooth
        + jnp.concatenate([smooth[:, 1:], smooth[:, :1]], axis=1)
        + jnp.concatenate([smooth[:, -1:], smooth[:, :-1]], axis=1)
    ).reshape(spectrum.shape)
    weighted = spectrum * root(smooth * (1.0 / 9.0))
    turned = []
    for d in range(dates):
        w = weighted[d * looks_az : (d + 1) * looks_az]
        w = jnp.concatenate([w[:, :WIN], w[:, WIN:]], axis=0)
        turned.append(rows_to_cols(dot_high(cols_fwd, w)))
    back = dot_high(jnp.concatenate(turned, axis=0), rows_fwd)
    squares = back * back
    power = dot_right(squares + pltpu.roll(squares, WIN, 1), blk_ref[2]).reshape(-1, PATCH, LANES)
    power = jnp.sum(power, axis=1, keepdims=True) * (1.0 / (PATCH * PATCH))
    scaled = back.reshape(-1, PATCH, LANES) * lax.rsqrt(power + RMS_EPS)
    scaled = scaled.reshape(back.shape)
    for d in range(dates):
        rows = scaled[d * looks_az : (d + 1) * looks_az]
        out_ref[d, 0] = rows[:, :WIN]
        out_ref[d, 1] = rows[:, WIN:]


def ring_device(position, count):
    half = count // 2
    return jnp.where(position < half, 2 * position, 2 * (count - 1 - position) + 1)


def kernel(
    at_ref, ct_ref, pr_ref, img_ref, dft_ref, blk_ref, azp_ref, rgp_ref,
    sim_ref, out_ref,
    image, halo, ref, wide, shifted, devs, band, prod, pooled, stats, sims,
    image_sem, root_sem, halo_send, halo_recv, ref_send, ref_recv,
):
    dates, _, lines, samples = img_ref.shape
    strips = samples // LANES
    rows = lines // WIN
    pieces = ref_send.shape[1]
    height = lines // pieces
    each = WIN // height
    count = lax.axis_size("date")
    az_count = lax.axis_size("az")
    az = lax.axis_index("az")
    mine = lax.axis_index("date")
    position = jnp.where(mine % 2 == 0, mine // 2, count - 1 - mine // 2)
    after = ring_device((position + 1) % count, count)
    before = ring_device((position + count - 1) % count, count)
    hops = (position, (count - position) % count)
    targets = (after, before)
    mesh_ids = pl.DeviceIdType.MESH

    def load(i):
        d = i // 2
        c = i % 2
        return pltpu.make_async_copy(img_ref.at[d, c], image.at[d, c], image_sem.at[i])

    for i in range(2 * dates):
        load(i).start()
    own = pltpu.make_async_copy(img_ref.at[0], ref, root_sem)

    @pl.when(mine == 0)
    def _():
        own.start()

    barrier = pltpu.get_barrier_semaphore()
    for target in targets:
        pl.semaphore_signal(barrier, inc=1, device_id={"date": target}, device_id_type=mesh_ids)

    @pl.when(az > 0)
    def _():
        pl.semaphore_signal(barrier, inc=1, device_id={"az": az - 1}, device_id_type=mesh_ids)

    @pl.when(az < az_count - 1)
    def _():
        pl.semaphore_signal(barrier, inc=1, device_id={"az": az + 1}, device_id_type=mesh_ids)

    peers = 2 + jnp.where(az > 0, 1, 0) + jnp.where(az < az_count - 1, 1, 0)
    pl.semaphore_wait(barrier, peers)

    def row_of(s):
        return jnp.where(s < rows - 2, s + 1, jnp.where(s == rows - 2, 0, rows - 1))

    def piece_rows(j):
        return pl.ds(pl.multiple_of(row_of(j // each) * WIN + (j % each) * height, height), height)

    def relay(c, j, first):
        at = piece_rows(j)
        return pltpu.make_async_remote_copy(
            src_ref=img_ref.at[0, c, at] if first else ref.at[c, at],
            dst_ref=ref.at[c, at],
            send_sem=ref_send.at[c, j],
            recv_sem=ref_recv.at[c, j],
            device_id={"date": targets[c]},
            device_id_type=mesh_ids,
        )

    def launch(j):
        for c in range(2):
            relay(c, j, True).start()

    def slot(t):
        for c in range(2):
            j = t - (hops[c] - 1) * LAG
            here = (hops[c] > 0) & (j >= 0) & (j < pieces)

            @pl.when(here)
            def _():
                relay(c, j, False).wait_recv()

            @pl.when(here & (hops[c] < count - 1))
            def _():
                relay(c, j, False).start()

        @pl.when((mine == 0) & (t + AHEAD < pieces))
        def _():
            launch(t + AHEAD)

    @pl.when(mine == 0)
    def _():
        for j in range(AHEAD):
            launch(j)

    def edge(k):
        start = 0 if k else lines - MARGIN
        return pltpu.make_async_remote_copy(
            src_ref=img_ref.at[:, :, pl.ds(start, MARGIN)],
            dst_ref=halo.at[k],
            send_sem=halo_send.at[k],
            recv_sem=halo_recv.at[k],
            device_id={"az": az - 1 if k else az + 1},
            device_id_type=mesh_ids,
        )

    sends = (az < az_count - 1, az > 0)
    takes = (az > 0, az < az_count - 1)
    for k in range(2):
        @pl.when(sends[k])
        def _():
            edge(k).start()

    def widen(i, carry):
        d = i // 2
        c = i % 2
        load(i).wait()
        for m in range(strips):
            cols = slice(m * LANES, (m + 1) * LANES)
            wide[d, c, m, MARGIN : MARGIN + lines, :] = image[d, c, :, cols].astype(F32)
            wide[d, c, m, 2 * MARGIN + lines : 2 * MARGIN + lines + WIN, :] = jnp.zeros((WIN, LANES), F32)

        @pl.when(i >= 2 * dates - opening)
        def _():
            slot(i - (2 * dates - opening))

        return carry

    early = each + (count - 2) * LAG
    opening = min(OPENING, 2 * dates)
    lax.fori_loop(0, 2 * dates, widen, 0)

    def fringe(k):
        first = MARGIN + lines if k else 0

        @pl.when(takes[k])
        def _():
            edge(k).wait_recv()

            def convert(i, carry):
                d = i // 2
                c = i % 2
                for m in range(strips):
                    cols = slice(m * LANES, (m + 1) * LANES)
                    wide[d, c, m, first : first + MARGIN, :] = halo[k, d, c, :, cols].astype(F32)
                return carry

            lax.fori_loop(0, 2 * dates, convert, 0)

        @pl.when(jnp.logical_not(takes[k]))
        def _():
            def clear(i, carry):
                for m in range(strips):
                    wide[i // 2, i % 2, m, first : first + MARGIN, :] = jnp.zeros((MARGIN, LANES), F32)
                return carry

            lax.fori_loop(0, 2 * dates, clear, 0)

    share = -(-(early - opening) // (dates * rows))
    pace = max(1, dates * rows // max(1, early - opening))

    def shift(i, carry):
        s = i // dates

        @pl.when((i % pace) == 0)
        def _():
            for e in range(share):
                t = opening + (i // pace) * share + e

                @pl.when(t < early)
                def _():
                    slot(t)

        @pl.when(i == (rows - 2) * dates)
        def _():
            for k in range(2):
                fringe(k)

        resample(row_of(s), i % dates, (dates, lines, strips), at_ref, ct_ref, pr_ref, wide, shifted, devs, stats)
        return carry

    lax.fori_loop(0, dates * rows, shift, 0)

    @pl.when(mine == 0)
    def _():
        own.wait()

    def row(s, carry):
        p = row_of(s)

        def ref_chunk(c, cols):
            return ref[c, pl.ds(pl.multiple_of(p * WIN, WIN), WIN), cols].astype(F32)

        def follow(d):
            share = -(-each // dates)
            for e in range(share):
                k = d * share + e

                @pl.when((s < rows - 1) & (k < each))
                def _():
                    slot(early + s * each + k)

        window_row(
            p, (dates, lines, strips), ref_chunk, blk_ref, rgp_ref,
            shifted, devs, band, prod, pooled, stats, sims, follow,
        )
        return carry

    lax.fori_loop(0, rows, row, 0)
    for p in range(rows):
        sim_ref[p] = sims[p].reshape(dates, LANES)[:, : sim_ref.shape[2]]
    goldstein(dates, out_ref, dft_ref, blk_ref, azp_ref, pooled)

    for c in range(2):
        @pl.when(hops[c] < count - 1)
        def _():
            def drain(j, carry):
                relay(c, j, False).wait_send()
                return carry

            lax.fori_loop(0, pieces, drain, 0)

    for k in range(2):
        @pl.when(sends[k])
        def _():
            edge(k).wait_send()


def on_device(image, along, cross, present):
    dates, _, lines, samples = image.shape
    strips = samples // LANES
    rows = lines // WIN
    pieces = lines // PIECE
    smem = pl.BlockSpec(memory_space=pltpu.SMEM)
    vmem = pl.BlockSpec(memory_space=pltpu.VMEM)
    dma = pltpu.SemaphoreType.DMA
    similarity, filtered = pl.pallas_call(
        kernel,
        out_shape=(
            jax.ShapeDtypeStruct((rows, dates, samples // WIN), F32),
            jax.ShapeDtypeStruct((dates, 2, lines // LOOK_AZ, samples // LOOK_RG), F32),
        ),
        in_specs=[smem] * 3 + [pl.BlockSpec(memory_space=pl.ANY)] + [vmem] * 4,
        out_specs=(vmem, vmem),
        scratch_shapes=[
            pltpu.VMEM((dates, 2, lines, samples), BF16),
            pltpu.VMEM((2, dates, 2, MARGIN, samples), BF16),
            pltpu.VMEM((2, lines, samples), BF16),
            pltpu.VMEM((dates, 2, strips, lines + 2 * MARGIN + WIN, LANES), F32),
            pltpu.VMEM((dates, 2, strips, lines, LANES), F32),
            pltpu.VMEM((dates, strips, lines, LANES), F32),
            pltpu.VMEM((3, strips, WIN, LANES), F32),
            pltpu.VMEM((dates, 2, WIN, 2 * samples), BF16),
            pltpu.VMEM((dates, 2, lines, samples // LOOK_RG), F32),
            pltpu.VMEM((rows, 3, strips, dates + 1, 8, LANES), F32),
            pltpu.VMEM((rows, dates, 1, LANES), F32),
            dma((2 * dates,)),
            dma(()),
            dma((2,)),
            dma((2,)),
            dma((2, pieces)),
            dma((2, pieces)),
        ],
        compiler_params=pltpu.CompilerParams(
            vmem_limit_bytes=62 * 1024 * 1024, collective_id=0, has_side_effects=True
        ),
    )(
        along.transpose(1, 0, 2), cross.transpose(1, 0, 2), present, image, *tables(lines, samples)
    )
    return similarity.transpose(1, 0, 2), filtered


def solution(mesh):
    placed = (
        P("date", None, "az", None),
        P("date", "az", None),
        P("date", "az", None),
        P("date", "az"),
    )
    return jax.shard_map(
        on_device,
        mesh=mesh,
        in_specs=placed,
        out_specs=(P("date", "az", None), P("date", None, "az", None)),
        check_vma=False,
    )
```

```python
import jax
import jax.numpy as jnp
import numpy as np
from jax import lax
from jax.experimental import pallas as pl
from jax.experimental.pallas import tpu as pltpu
from jax.sharding import PartitionSpec as P

WIN = 64
MARGIN = 32
LOOK_AZ = 5
LOOK_RG = 20
PATCH = 32
LANES = 128
PIECE = 16
AHEAD = 8
LAG = 5
OPENING = 4

VAR_EPS = 1e-05
RMS_EPS = 1e-06
TINY = 1e-37

F32 = jnp.float32
BF16 = jnp.bfloat16


def tables(lines, samples):
    turns = np.outer(np.arange(PATCH), np.arange(PATCH)) % PATCH
    angles = turns * (2.0 * np.pi / PATCH)
    two = np.eye(2)
    cosine = np.kron(two, np.cos(angles))
    sine = np.kron(two, np.sin(angles))
    rows_fwd = np.block([[cosine, sine], [-sine, cosine]])
    cols_fwd = np.block([[cosine, -sine], [sine, cosine]])
    dft = np.stack([rows_fwd, cols_fwd]).astype(np.float32)
    near = np.abs(np.arange(PATCH)[:, None] - np.arange(PATCH)[None, :])
    circular = np.minimum(near, PATCH - near) <= 1
    four = np.eye(LANES // PATCH)
    half = np.kron(np.eye(2), np.ones((WIN, WIN)))
    blocks = np.stack(
        [half, np.kron(four, circular), np.kron(four, np.ones((PATCH, PATCH)))]
    ).astype(np.float32)
    az_pool = (
        np.arange(lines // LOOK_AZ)[:, None] == np.arange(lines)[None, :] // LOOK_AZ
    ).astype(np.float32)
    rg_pool = (
        np.arange(samples)[:, None] // LOOK_RG == np.arange(samples // LOOK_RG)[None, :]
    ).astype(np.float32)
    rg_pool = np.concatenate([rg_pool, rg_pool], axis=0)
    return (
        jnp.asarray(dft),
        jnp.asarray(blocks, BF16),
        jnp.asarray(az_pool, BF16),
        jnp.asarray(rg_pool, BF16),
    )


def dot(a, b):
    return jnp.dot(a, b, preferred_element_type=F32)


def dot_high(a, b):
    a_high, a_low = split(a)
    b_high, b_low = split(b)
    return dot(a_high, b_high) + (dot(a_high, b_low) + dot(a_low, b_high))


def split(x):
    high = x.astype(BF16)
    return high, (x - high.astype(F32)).astype(BF16)


def dot_right(x, ones):
    high, low = split(x)
    return dot(high, ones) + dot(low, ones)


def dot_left(ones, x):
    high, low = split(x)
    return dot(ones, high) + dot(ones, low)


def root(x):
    return x * lax.rsqrt(jnp.maximum(x, TINY))


def resample(p, d, sizes, at_ref, ct_ref, pr_ref, wide, shifted, devs, stats):
    dates, lines, strips = sizes
    lane = lax.broadcasted_iota(jnp.int32, (WIN, LANES), 1)
    first = lane < WIN
    near_low = lane < LANES - MARGIN
    near_high = lane < MARGIN
    present = pr_ref[d, p]
    here = pl.ds(pl.multiple_of(p * WIN, WIN), WIN)
    for m in range(strips):
        rows = []
        turns = []
        for q in (2 * m, 2 * m + 1):
            start = jnp.where(
                present != 0, p * WIN + MARGIN + at_ref[p, d, q], lines + 2 * MARGIN
            )
            rows.append(pl.ds(start, WIN))
            turns.append((LANES - ct_ref[p, d, q]) % LANES)
        part = []
        for c in range(2):
            even = wide[d, c, m, rows[0], :]
            below = wide[d, c, m - 1, rows[0], :] if m > 0 else jnp.zeros_like(even)
            odd = wide[d, c, m, rows[1], :]
            above = wide[d, c, m + 1, rows[1], :] if m + 1 < strips else jnp.zeros_like(odd)
            even = pltpu.roll(jnp.where(near_low, even, below), turns[0], 1)
            odd = pltpu.roll(jnp.where(near_high, above, odd), turns[1], 1)
            part.append(jnp.where(first, even, odd))
            shifted[d, c, m, here, :] = part[c]
        amp = root(part[0] * part[0] + part[1] * part[1]).reshape(WIN // 8, 8, LANES)
        mean = jnp.sum(amp, axis=0) * (8.0 / WIN)
        dev = amp - mean[None]
        devs[d, m, here, :] = dev.reshape(WIN, LANES)
        stats[p, 0, m, d] = mean
        stats[p, 1, m, d] = jnp.sum(dev * dev, axis=0)


def window_row(p, sizes, ref_chunk, blk_ref, rgp_ref, shifted, devs, band, prod, pooled, stats, sims, follow):
    dates, lines, strips = sizes
    for m in range(strips):
        cols = slice(m * LANES, (m + 1) * LANES)
        real = ref_chunk(0, cols)
        imag = ref_chunk(1, cols)
        band[0, m] = real
        band[1, m] = imag
        amp = root(real * real + imag * imag).reshape(WIN // 8, 8, LANES)
        mean = jnp.sum(amp, axis=0) * (8.0 / WIN)
        dev = amp - mean[None]
        band[2, m] = dev.reshape(WIN, LANES)
        stats[p, 0, m, dates] = mean
        stats[p, 1, m, dates] = jnp.sum(dev * dev, axis=0)

    def one_date(d, carry):
        follow(d)
        here = pl.ds(pl.multiple_of(p * WIN, WIN), WIN)
        for m in range(strips):
            sr = shifted[d, 0, m, here, :]
            si = shifted[d, 1, m, here, :]
            joint = devs[d, m, here, :] * band[2, m]
            stats[p, 2, m, d] = jnp.sum(joint.reshape(WIN // 8, 8, LANES), axis=0)
            rr = band[0, m]
            ri = band[1, m]
            for c, value in enumerate((rr * sr + ri * si, ri * sr - rr * si)):
                high, low = split(value)
                prod[d, c, :, m * LANES : (m + 1) * LANES] = high
                prod[d, c, :, (strips + m) * LANES : (strips + m + 1) * LANES] = low
        return carry

    lax.fori_loop(0, dates, one_date, 0)
    width = 2 * strips * LANES
    sums = dot(prod[...].reshape(dates * 2 * WIN, width), rgp_ref[...])
    pooled[:, :, pl.ds(pl.multiple_of(p * WIN, WIN), WIN), :] = sums.reshape(dates, 2, WIN, -1)

    half = blk_ref[0]

    def total(x):
        flat = x.reshape(-1, LANES)
        return jnp.sum(dot_right(flat, half).reshape(-1, 8, LANES), axis=1, keepdims=True)

    count = 8.0 * WIN
    means = stats[p, 0].reshape(strips * (dates + 1), 8, LANES)
    away = means - total(means) * (1.0 / count)
    spread = stats[p, 1].reshape(strips * (dates + 1), 8, LANES)
    var = total(spread + (WIN / 8.0) * (away * away)) * (1.0 / (WIN * WIN))
    away = away.reshape(strips, dates + 1, 8, LANES)
    var = var.reshape(strips, dates + 1, 1, LANES)
    joint = stats[p, 2][:, :dates] + (WIN / 8.0) * (away[:, :dates] * away[:, dates:])
    cov = total(joint).reshape(strips, dates, 1, LANES) * (1.0 / (WIN * WIN))
    corr = cov / jnp.sqrt((var[:, dates:] + VAR_EPS) * (var[:, :dates] + VAR_EPS))
    lane = lax.broadcasted_iota(jnp.int32, (dates, 1, LANES), 2)
    found = jnp.zeros((dates, 1, LANES), F32)
    for m in range(strips):
        here = corr[m]
        other = pltpu.roll(here.reshape(dates, LANES), WIN, 1).reshape(dates, 1, LANES)
        left = jnp.where(lane < WIN, here, other)
        right = jnp.where(lane < WIN, other, here)
        found = jnp.where(lane == 2 * m, left, jnp.where(lane == 2 * m + 1, right, found))
    sims[p] = found


def goldstein(dates, out_ref, dft_ref, blk_ref, azp_ref, pooled):
    az_pool = azp_ref[...]
    looks_az = az_pool.shape[0]
    rows_fwd = dft_ref[0]
    cols_fwd = dft_ref[1]

    def rows_to_cols(x):
        return jnp.concatenate([x[:looks_az], x[looks_az:]], axis=1)

    turned = []
    for d in range(dates):
        z = jnp.concatenate([dot_left(az_pool, pooled[d, c]) for c in range(2)], axis=0)
        turned.append(rows_to_cols(dot_high(rows_fwd, z)))
    spectrum = dot_high(jnp.concatenate(turned, axis=0), cols_fwd)
    squares = spectrum * spectrum
    magnitude = root(squares + pltpu.roll(squares, WIN, 1))
    smooth = dot_right(magnitude, blk_ref[1]).reshape(-1, PATCH, LANES)
    smooth = (
        smooth
        + jnp.concatenate([smooth[:, 1:], smooth[:, :1]], axis=1)
        + jnp.concatenate([smooth[:, -1:], smooth[:, :-1]], axis=1)
    ).reshape(spectrum.shape)
    weighted = spectrum * root(smooth * (1.0 / 9.0))
    turned = []
    for d in range(dates):
        w = weighted[d * looks_az : (d + 1) * looks_az]
        w = jnp.concatenate([w[:, :WIN], w[:, WIN:]], axis=0)
        turned.append(rows_to_cols(dot_high(cols_fwd, w)))
    back = dot_high(jnp.concatenate(turned, axis=0), rows_fwd)
    squares = back * back
    power = dot_right(squares + pltpu.roll(squares, WIN, 1), blk_ref[2]).reshape(-1, PATCH, LANES)
    power = jnp.sum(power, axis=1, keepdims=True) * (1.0 / (PATCH * PATCH))
    scaled = back.reshape(-1, PATCH, LANES) * lax.rsqrt(power + RMS_EPS)
    scaled = scaled.reshape(back.shape)
    for d in range(dates):
        rows = scaled[d * looks_az : (d + 1) * looks_az]
        out_ref[d, 0] = rows[:, :WIN]
        out_ref[d, 1] = rows[:, WIN:]


def ring_device(position, count):
    half = count // 2
    return jnp.where(position < half, 2 * position, 2 * (count - 1 - position) + 1)


def kernel(
    at_ref, ct_ref, pr_ref, img_ref, blk_ref, rgp_ref,
    sim_ref, pooled,
    image, halo, ref, wide, shifted, devs, band, prod, stats, sims,
    image_sem, root_sem, halo_send, halo_recv, ref_send, ref_recv,
):
    dates, _, lines, samples = img_ref.shape
    strips = samples // LANES
    rows = lines // WIN
    pieces = ref_send.shape[1]
    height = lines // pieces
    each = WIN // height
    count = lax.axis_size("date")
    az_count = lax.axis_size("az")
    az = lax.axis_index("az")
    mine = lax.axis_index("date")
    position = jnp.where(mine % 2 == 0, mine // 2, count - 1 - mine // 2)
    after = ring_device((position + 1) % count, count)
    before = ring_device((position + count - 1) % count, count)
    hops = (position, (count - position) % count)
    targets = (after, before)
    mesh_ids = pl.DeviceIdType.MESH

    def load(i):
        d = i // 2
        c = i % 2
        return pltpu.make_async_copy(img_ref.at[d, c], image.at[d, c], image_sem.at[i])

    for i in range(2 * dates):
        load(i).start()
    own = pltpu.make_async_copy(img_ref.at[0], ref, root_sem)

    @pl.when(mine == 0)
    def _():
        own.start()

    barrier = pltpu.get_barrier_semaphore()
    for target in targets:
        pl.semaphore_signal(barrier, inc=1, device_id={"date": target}, device_id_type=mesh_ids)

    @pl.when(az > 0)
    def _():
        pl.semaphore_signal(barrier, inc=1, device_id={"az": az - 1}, device_id_type=mesh_ids)

    @pl.when(az < az_count - 1)
    def _():
        pl.semaphore_signal(barrier, inc=1, device_id={"az": az + 1}, device_id_type=mesh_ids)

    peers = 2 + jnp.where(az > 0, 1, 0) + jnp.where(az < az_count - 1, 1, 0)
    pl.semaphore_wait(barrier, peers)

    def row_of(s):
        return jnp.where(s < rows - 2, s + 1, jnp.where(s == rows - 2, 0, rows - 1))

    def piece_rows(j):
        return pl.ds(pl.multiple_of(row_of(j // each) * WIN + (j % each) * height, height), height)

    def relay(c, j, first):
        at = piece_rows(j)
        return pltpu.make_async_remote_copy(
            src_ref=img_ref.at[0, c, at] if first else ref.at[c, at],
            dst_ref=ref.at[c, at],
            send_sem=ref_send.at[c, j],
            recv_sem=ref_recv.at[c, j],
            device_id={"date": targets[c]},
            device_id_type=mesh_ids,
        )

    def launch(j):
        for c in range(2):
            relay(c, j, True).start()

    def slot(t):
        for c in range(2):
            j = t - (hops[c] - 1) * LAG
            here = (hops[c] > 0) & (j >= 0) & (j < pieces)

            @pl.when(here)
            def _():
                relay(c, j, False).wait_recv()

            @pl.when(here & (hops[c] < count - 1))
            def _():
                relay(c, j, False).start()

        @pl.when((mine == 0) & (t + AHEAD < pieces))
        def _():
            launch(t + AHEAD)

    @pl.when(mine == 0)
    def _():
        for j in range(AHEAD):
            launch(j)

    def edge(k):
        start = 0 if k else lines - MARGIN
        return pltpu.make_async_remote_copy(
            src_ref=img_ref.at[:, :, pl.ds(start, MARGIN)],
            dst_ref=halo.at[k],
            send_sem=halo_send.at[k],
            recv_sem=halo_recv.at[k],
            device_id={"az": az - 1 if k else az + 1},
            device_id_type=mesh_ids,
        )

    sends = (az < az_count - 1, az > 0)
    takes = (az > 0, az < az_count - 1)
    for k in range(2):
        @pl.when(sends[k])
        def _():
            edge(k).start()

    def widen(i, carry):
        d = i // 2
        c = i % 2
        load(i).wait()
        for m in range(strips):
            cols = slice(m * LANES, (m + 1) * LANES)
            wide[d, c, m, MARGIN : MARGIN + lines, :] = image[d, c, :, cols].astype(F32)
            wide[d, c, m, 2 * MARGIN + lines : 2 * MARGIN + lines + WIN, :] = jnp.zeros((WIN, LANES), F32)

        @pl.when(i >= 2 * dates - opening)
        def _():
            slot(i - (2 * dates - opening))

        return carry

    early = each + (count - 2) * LAG
    opening = min(OPENING, 2 * dates)
    lax.fori_loop(0, 2 * dates, widen, 0)

    def fringe(k):
        first = MARGIN + lines if k else 0

        @pl.when(takes[k])
        def _():
            edge(k).wait_recv()

            def convert(i, carry):
                d = i // 2
                c = i % 2
                for m in range(strips):
                    cols = slice(m * LANES, (m + 1) * LANES)
                    wide[d, c, m, first : first + MARGIN, :] = halo[k, d, c, :, cols].astype(F32)
                return carry

            lax.fori_loop(0, 2 * dates, convert, 0)

        @pl.when(jnp.logical_not(takes[k]))
        def _():
            def clear(i, carry):
                for m in range(strips):
                    wide[i // 2, i % 2, m, first : first + MARGIN, :] = jnp.zeros((MARGIN, LANES), F32)
                return carry

            lax.fori_loop(0, 2 * dates, clear, 0)

    share = -(-(early - opening) // (dates * rows))
    pace = max(1, dates * rows // max(1, early - opening))

    def shift(i, carry):
        s = i // dates

        @pl.when((i % pace) == 0)
        def _():
            for e in range(share):
                t = opening + (i // pace) * share + e

                @pl.when(t < early)
                def _():
                    slot(t)

        @pl.when(i == (rows - 2) * dates)
        def _():
            for k in range(2):
                fringe(k)

        resample(row_of(s), i % dates, (dates, lines, strips), at_ref, ct_ref, pr_ref, wide, shifted, devs, stats)
        return carry

    lax.fori_loop(0, dates * rows, shift, 0)

    @pl.when(mine == 0)
    def _():
        own.wait()

    def row(s, carry):
        p = row_of(s)

        def ref_chunk(c, cols):
            return ref[c, pl.ds(pl.multiple_of(p * WIN, WIN), WIN), cols].astype(F32)

        def follow(d):
            share = -(-each // dates)
            for e in range(share):
                k = d * share + e

                @pl.when((s < rows - 1) & (k < each))
                def _():
                    slot(early + s * each + k)

        window_row(
            p, (dates, lines, strips), ref_chunk, blk_ref, rgp_ref,
            shifted, devs, band, prod, pooled, stats, sims, follow,
        )
        return carry

    lax.fori_loop(0, rows, row, 0)
    for p in range(rows):
        sim_ref[p] = sims[p].reshape(dates, LANES)[:, : sim_ref.shape[2]]

    for c in range(2):
        @pl.when(hops[c] < count - 1)
        def _():
            def drain(j, carry):
                relay(c, j, False).wait_send()
                return carry

            lax.fori_loop(0, pieces, drain, 0)

    for k in range(2):
        @pl.when(sends[k])
        def _():
            edge(k).wait_send()


def finish(found_ref, pooled_ref, dft_ref, blk_ref, azp_ref, sim_ref, out_ref):
    sim_ref[...] = found_ref[...]
    goldstein(out_ref.shape[0], out_ref, dft_ref, blk_ref, azp_ref, pooled_ref)


def on_device(image, along, cross, present):
    dates, _, lines, samples = image.shape
    strips = samples // LANES
    rows = lines // WIN
    pieces = lines // PIECE
    smem = pl.BlockSpec(memory_space=pltpu.SMEM)
    vmem = pl.BlockSpec(memory_space=pltpu.VMEM)
    dma = pltpu.SemaphoreType.DMA
    dft, blocks, az_pool, rg_pool = tables(lines, samples)
    similarity, pooled = pl.pallas_call(
        kernel,
        out_shape=(
            jax.ShapeDtypeStruct((rows, dates, samples // WIN), F32),
            jax.ShapeDtypeStruct((dates, 2, lines, samples // LOOK_RG), F32),
        ),
        in_specs=[smem] * 3 + [pl.BlockSpec(memory_space=pl.ANY)] + [vmem] * 2,
        out_specs=(vmem, vmem),
        scratch_shapes=[
            pltpu.VMEM((dates, 2, lines, samples), BF16),
            pltpu.VMEM((2, dates, 2, MARGIN, samples), BF16),
            pltpu.VMEM((2, lines, samples), BF16),
            pltpu.VMEM((dates, 2, strips, lines + 2 * MARGIN + WIN, LANES), F32),
            pltpu.VMEM((dates, 2, strips, lines, LANES), F32),
            pltpu.VMEM((dates, strips, lines, LANES), F32),
            pltpu.VMEM((3, strips, WIN, LANES), F32),
            pltpu.VMEM((dates, 2, WIN, 2 * samples), BF16),
            pltpu.VMEM((rows, 3, strips, dates + 1, 8, LANES), F32),
            pltpu.VMEM((rows, dates, 1, LANES), F32),
            dma((2 * dates,)),
            dma(()),
            dma((2,)),
            dma((2,)),
            dma((2, pieces)),
            dma((2, pieces)),
        ],
        compiler_params=pltpu.CompilerParams(
            vmem_limit_bytes=62 * 1024 * 1024, collective_id=0, has_side_effects=True
        ),
    )(
        along.transpose(1, 0, 2), cross.transpose(1, 0, 2), present, image, blocks, rg_pool
    )
    similarity, filtered = pl.pallas_call(
        finish,
        out_shape=(
            jax.ShapeDtypeStruct(similarity.shape, F32),
            jax.ShapeDtypeStruct((dates, 2, lines // LOOK_AZ, samples // LOOK_RG), F32),
        ),
        in_specs=[vmem] * 5,
        out_specs=(vmem, vmem),
    )(similarity, pooled, dft, blocks, az_pool)
    return similarity.transpose(1, 0, 2), filtered


def solution(mesh):
    placed = (
        P("date", None, "az", None),
        P("date", "az", None),
        P("date", "az", None),
        P("date", "az"),
    )
    return jax.shard_map(
        on_device,
        mesh=mesh,
        in_specs=placed,
        out_specs=(P("date", "az", None), P("date", None, "az", None)),
        check_vma=False,
    )
```
